32 devices in a mesh: space: 16 (over z, y, x), slab: 2 (over core).
Axes of the slice: x: 2, y: 2, z: 4, core: 2. Of those that a mesh axis runs over, the one named last changes fastest.
Arguments:
- phases: float32 [8, 192, 24, 384], P(None, 'space', 'slab'), may hold values from 0 to 1
- mobility: float32 [8], replicated, may hold values from 0.02 to 0.08
- active: int32 [16, 2, 32, 8], P('space', 'slab'), may hold values from 0 to 1, as said below
- variants: float32 [8, 3], replicated, may hold values from -4 to 4
Outputs:
- evolved: float32 [8, 192, 24, 384], P(None, 'space', 'slab')
- displacement: float32 [3, 384, 24, 192], P(None, 'space', 'slab')
The draws below stay inside these ranges and needn't reach their ends.
Inputs may be any that keep to these rules, and one draw needn't show every extreme that they name: 1 marks an order parameter that evolves in that brick; the share of active ones differs strongly between brick indices along the first dimension.
All inputs are finite; a program needn't handle non-finite values.
Results may differ from the reference program's by a relative error of at most 0.00016.
Values sent between devices are 32-bit elements; how exact they have to be, the bound alone decides.
A program may use at most 128 MiB of HBM per device.

```python
import math
import jax
import jax.numpy as jnp
from jax import lax

P_SIZE = 8
BRICK = 12
STEPS = 3
ITERS = 4
NI = 192
NJ = 24
NK = 384


def draw_active(key, part):
    rows_first = NI // BRICK
    rows_second = NJ // BRICK
    rows_third = NK // BRICK
    order_key, score_key = jax.random.split(jax.random.fold_in(key, 7))
    ranking = jax.random.permutation(order_key, rows_first).astype(jnp.int32)
    highest = max(rows_first - 1, 1)
    cutoff = 50 + 950 * (ranking * ranking // highest) * ranking // highest // highest
    scores = jax.random.randint(score_key, (rows_first, rows_second, rows_third, P_SIZE), 0, 1000)
    return (scores < cutoff[:, None, None, None]).astype(jnp.int32)


def block_scale(rng, shape, pieces, smallest, high):
    def one(axis_at, shards_of):
        draws = jax.random.uniform(jax.random.fold_in(jax.random.fold_in(rng, 6), axis_at), (shards_of,), jnp.float32, smallest / len(pieces), high / len(pieces))
        return jnp.repeat(jnp.exp(draws), shape[axis_at] // shards_of).reshape((-1,) + (1,) * (len(shape) - axis_at - 1))

    loudness = one(*pieces[0])
    for cut in pieces[1:]:
        loudness = loudness * one(*cut)
    return loudness


def normal_values(key, extent, spread, most, held_as=jnp.bfloat16):
    return jnp.clip(spread * jax.random.normal(key, extent, jnp.float32), -most, most).astype(held_as)


def setup_inputs(seed: int = 0) -> dict:
    arg_keys = jax.random.split(jax.random.key(seed), 5)
    phases = jnp.clip(1.0 * jax.random.uniform(arg_keys[0], (P_SIZE, NI, NJ, NK), jnp.float32) ** block_scale(arg_keys[0], (P_SIZE, NI, NJ, NK), ((1, 16), (2, 2)), -0.2, 0.2), 0.0, 1.0)
    mobility = jnp.clip(jnp.exp(jax.random.uniform(arg_keys[1], (P_SIZE,), jnp.float32, math.log(0.02), math.log(0.08))), 0.02, 0.08)
    active = draw_active(jax.random.fold_in(arg_keys[4], 71), 0)
    variants = normal_values(arg_keys[3], (P_SIZE, 3), 1.0, 4.0, jnp.float32)
    return {"phases": phases, "mobility": mobility, "active": active, "variants": variants}


PAIR_ENERGY = 1.5
DIAGONAL_SHIFT = 3.0
SPECTRUM_CENTRE = 12.0
SPECTRUM_RADIUS = 9.0


def relax(fields, padded, speeds):
    summed = (padded[:, 2:, 1:-1, 1:-1] + padded[:, :-2, 1:-1, 1:-1] + padded[:, 1:-1, 2:, 1:-1]
              + padded[:, 1:-1, :-2, 1:-1] + padded[:, 1:-1, 1:-1, 2:] + padded[:, 1:-1, 1:-1, :-2])
    laplace = summed - 6.0 * fields
    squares = jnp.sum(fields * fields, axis=0)
    driving = fields * fields * fields - fields + 2.0 * PAIR_ENERGY * fields * (squares - fields * fields) - laplace
    return fields - speeds * driving


def coefficients(fields, variants):
    squared = fields * fields
    summed = jnp.sum(squared, axis=0)
    saturation = summed / (1.0 + summed)
    excess = 0.5 * saturation
    lame_first = 1.5 + saturation
    strain = jnp.einsum("pabc,pk->kabc", squared, variants, precision=lax.Precision.HIGHEST)
    dilation = strain[0] + strain[1] + strain[2]
    stress = lame_first * dilation + 2.0 * (1.0 + excess) * strain
    return jnp.concatenate([excess[None], stress], axis=0)


def shifted(padded, along, offset):
    slicer = [slice(None)] * padded.ndim
    for dimension in range(padded.ndim - 3, padded.ndim):
        lowest = 1 + (offset if dimension == padded.ndim + along else 0)
        slicer[dimension] = slice(lowest, padded.shape[dimension] - 2 + lowest)
    return padded[tuple(slicer)]


def stiffness(padded, excess_pad):
    centre = shifted(padded, -1, 0)
    excess = shifted(excess_pad, -1, 0)
    summed = DIAGONAL_SHIFT * centre
    for along in (-3, -2, -1):
        for offset in (-1, 1):
            weight = 1.0 + 0.5 * (excess + shifted(excess_pad, along, offset))
            summed = summed + weight * (centre - shifted(padded, along, offset))
    return summed


def chebyshev(forcing, operate):
    ratio_now = SPECTRUM_RADIUS / SPECTRUM_CENTRE
    residual = forcing
    direction = forcing / SPECTRUM_CENTRE
    solution = jnp.zeros_like(forcing)
    for counter in range(ITERS):
        solution = solution + direction
        residual = residual - operate(direction)
        ratio_next = 1.0 / (2.0 * SPECTRUM_CENTRE / SPECTRUM_RADIUS - ratio_now)
        direction = ratio_next * ratio_now * direction + (2.0 * ratio_next / SPECTRUM_RADIUS) * residual
        ratio_now = ratio_next
    return solution + direction


def reference(phases, mobility, active, variants):
    flags = jnp.transpose(active.astype(jnp.float32), (3, 0, 1, 2))
    flags = jnp.repeat(jnp.repeat(jnp.repeat(flags, BRICK, axis=1), BRICK, axis=2), BRICK, axis=3)
    speeds = mobility[:, None, None, None] * flags
    fields = phases
    for counter in range(STEPS):
        padded = jnp.pad(fields, ((0, 0), (1, 1), (1, 1), (1, 1)))
        fields = relax(fields, padded, speeds)
    owned = coefficients(jnp.transpose(fields, (0, 3, 2, 1)), variants)
    padded = jnp.pad(owned, ((0, 0), (1, 1), (1, 1), (1, 1)))
    excess_pad = padded[0]
    forcing = jnp.stack([0.5 * (shifted(padded[1 + component], along, 1) - shifted(padded[1 + component], along, -1))
                         for component, along in enumerate((-1, -2, -3))])

    def operate(direction):
        return stiffness(jnp.pad(direction, ((0, 0), (1, 1), (1, 1), (1, 1))), excess_pad)

    return fields, chebyshev(forcing, operate)
```

```python
import functools

import jax
import jax.numpy as jnp
from jax import lax
from jax.experimental import pallas as pl
from jax.experimental.pallas import tpu as pltpu
from jax.sharding import PartitionSpec as P

STEPS = 3
ITERS = 4
PAIR_ENERGY = 1.5
DIAGONAL_SHIFT = 3.0
CENTRE = 12.0
RADIUS = 9.0


def ratios():
    now = RADIUS / CENTRE
    out = []
    for _ in range(ITERS):
        later = 1.0 / (2.0 * CENTRE / RADIUS - now)
        out.append((later * now, 2.0 * later / RADIUS))
        now = later
    return out


def kernel(
    sizes,
    phases,
    speeds,
    variants,
    evolved,
    moved,
    field_a,
    field_b,
    coef,
    stress_k,
    weights,
    diagonal,
    dir_a,
    dir_b,
    residual,
    total,
    flat,
    fsi,
    fri,
    fsj,
    frj,
    csi,
    cri,
    csj,
    crj,
    dsi,
    dri,
    dsj,
    drj,
    send_sem,
    recv_sem,
):
    ns, nl, np_, ni, nj, nk, jp = sizes
    space, slab = lax.axis_index("space"), lax.axis_index("slab")
    targets = (
        (space < ns - 1, {"space": jnp.minimum(space + 1, ns - 1)}),
        (space > 0, {"space": jnp.maximum(space - 1, 0)}),
        (slab < nl - 1, {"slab": jnp.minimum(slab + 1, nl - 1)}),
        (slab > 0, {"slab": jnp.maximum(slab - 1, 0)}),
    )
    barrier = pltpu.get_barrier_semaphore()
    for has, where in targets:

        @pl.when(has)
        def _(where=where):
            pl.semaphore_signal(
                barrier, inc=1, device_id=where, device_id_type=pl.DeviceIdType.MESH
            )

    peers = jnp.minimum(space, 1) + jnp.minimum(ns - 1 - space, 1)
    peers = peers + jnp.minimum(slab, 1) + jnp.minimum(nl - 1 - slab, 1)
    pl.semaphore_wait(barrier, peers)

    def buffers(stage):
        if stage < STEPS:
            return fsi.at[stage], fri.at[stage], fsj.at[stage], frj.at[stage]
        if stage == STEPS:
            return csi, cri, csj, crj
        at = stage - STEPS - 1
        return dsi.at[at], dri.at[at], dsj.at[at], drj.at[at]

    def copy(stage, way):
        si, ri, sj, rj = buffers(stage)
        source, landing = (si, ri) if way < 2 else (sj, rj)
        return pltpu.make_async_remote_copy(
            src_ref=source.at[way % 2],
            dst_ref=landing.at[way % 2],
            send_sem=send_sem.at[stage, way],
            recv_sem=recv_sem.at[stage, way],
            device_id=targets[way][1],
            device_id_type=pl.DeviceIdType.MESH,
        )

    def send_i(stage, read):
        count, si = read(0)[0], buffers(stage)[0]
        for side in (0, 1):

            @pl.when(targets[side][0])
            def _(side=side):
                plane = ni if side == 0 else 1
                for p in range(count):
                    si[side, p * nj : (p + 1) * nj, :] = read(p)[1](plane)
                copy(stage, side).start()

    def send_j(stage, read):
        count, sj = read(0)[0], buffers(stage)[2]
        for side in (0, 1):

            @pl.when(targets[2 + side][0])
            def _(side=side):
                row = nj - 1 if side == 0 else 0

                def body(i, _):
                    for p in range(count):
                        sj[side, i, p : p + 1, :] = read(p)[2](i + 1, row)
                    return 0

                lax.fori_loop(0, ni, body, 0)
                copy(stage, 2 + side).start()

    def take_i(stage, write):
        count, ri = write(0)[0], buffers(stage)[1]
        for side in (0, 1):

            @pl.when(targets[1 - side][0])
            def _(side=side):
                copy(stage, side).wait_recv()
                plane = 0 if side == 0 else ni + 1
                for p in range(count):
                    write(p)[1](plane, ri[side, p * nj : (p + 1) * nj, :])

    def take_j(stage, write):
        count, rj = write(0)[0], buffers(stage)[3]
        for side in (0, 1):

            @pl.when(targets[3 - side][0])
            def _(side=side):
                copy(stage, 2 + side).wait_recv()
                row = jp - 1 if side == 0 else nj

                def body(i, _):
                    for p in range(count):
                        write(p)[2](i + 1, row, rj[side, i, p : p + 1, :])
                    return 0

                lax.fori_loop(0, ni, body, 0)

    def reader(ref, count, slots_i=None, slots_j=None):
        def read(p):
            pi = slots_i[p] if slots_i else p
            pj = slots_j[p] if slots_j else p
            return (
                count,
                lambda plane: ref[plane, pi, 0:nj, :],
                lambda plane, row: ref[plane, pj, row : row + 1, :],
            )

        return read

    def writer(ref, count, slots_i=None, slots_j=None):
        def write(p):
            pi = slots_i[p] if slots_i else p
            pj = slots_j[p] if slots_j else p

            def whole(plane, value):
                ref[plane, pi, 0:nj, :] = value

            def line(plane, row, value):
                ref[plane, pj, row : row + 1, :] = value

            return count, whole, line

        return write

    def stage_in(i, _):
        for p in range(np_):
            field_a[i + 1, p, 0:nj, :] = phases[p, i]
        return 0

    lax.fori_loop(0, ni, stage_in, 0)
    send_i(0, reader(field_a, np_))
    send_j(0, reader(field_a, np_))
    for ref in (field_a, field_b, coef, dir_a, dir_b):
        count = ref.shape[1]
        blank = jnp.zeros((jp, nk), jnp.float32)
        for p in range(count):
            ref[0, p] = blank
            ref[ni + 1, p] = blank

        def clear(i, _, ref=ref, count=count):
            for p in range(count):
                ref[i + 1, p, nj:jp, :] = jnp.zeros((jp - nj, nk), jnp.float32)
            return 0

        lax.fori_loop(0, ni, clear, 0)
    flat[...] = jnp.zeros_like(flat)

    lane = lax.broadcasted_iota(jnp.int32, (jp, nk), 1)
    first, last = lane == 0, lane == nk - 1

    def up(x):
        return pltpu.roll(x, jp - 1, 0)

    def down(x):
        return pltpu.roll(x, 1, 0)

    def after(x):
        return pltpu.roll(x, nk - 1, 1)

    def before(x):
        return pltpu.roll(x, 1, 1)

    def relax(i, src, store):
        squares = None
        for p in range(np_):
            x = src[i, p]
            squares = x * x if squares is None else squares + x * x
        scaled = 2.0 * PAIR_ENERGY * squares + 5.0
        for p in range(np_):
            x = src[i, p]
            around = src[i + 1, p] + src[i - 1, p] + up(x) + down(x)
            around = around + jnp.where(last, 0.0, after(x)) + jnp.where(first, 0.0, before(x))
            driving = x * (scaled + (1.0 - 2.0 * PAIR_ENERGY) * (x * x)) - around
            store(i, p, x - speeds[p : p + 1, :] * driving)

    def run(plane, stage, write):
        take_j(stage, write)
        lax.fori_loop(2, ni, lambda i, _: (plane(i), 0)[1], 0)
        take_i(stage, write)
        plane(1)
        plane(ni)

    pair = (field_a, field_b)
    for step in range(STEPS - 1):
        src, dst = pair[step % 2], pair[(step + 1) % 2]

        def store(i, p, value, dst=dst):
            dst[i, p, 0:nj, :] = value[0:nj]

        run(lambda i, src=src, store=store: relax(i, src, store), step, writer(src, np_))
        send_i(step + 1, reader(dst, np_))
        send_j(step + 1, reader(dst, np_))

    src = pair[(STEPS - 1) % 2]

    def finish(i):
        sums = [None] * 4

        def store(i, p, value):
            evolved[p, i - 1] = value[0:nj]
            square = value * value
            terms = [square] + [square * variants[p, c] for c in range(3)]
            for at, term in enumerate(terms):
                sums[at] = term if sums[at] is None else sums[at] + term

        relax(i, src, store)
        saturation = sums[0] / (1.0 + sums[0])
        excess = 0.5 * saturation
        common = (1.5 + saturation) * (sums[1] + sums[2] + sums[3])
        twice = 2.0 * (1.0 + excess)
        coef[i, 0, 0:nj, :] = excess[0:nj]
        coef[i, 1, 0:nj, :] = (common + twice * sums[1])[0:nj]
        coef[i, 2, 0:nj, :] = (common + twice * sums[2])[0:nj]
        stress_k[i] = common + twice * sums[3]

    run(finish, STEPS - 1, writer(src, np_))
    send_i(STEPS, reader(coef, 2, (0, 1), (0, 2)))
    send_j(STEPS, reader(coef, 2, (0, 1), (0, 2)))

    def prepare(i):
        excess = coef[i, 0]
        own = 1.0 + 0.5 * excess
        around = [
            coef[i + 1, 0],
            coef[i - 1, 0],
            up(excess),
            down(excess),
            jnp.where(last, 0.0, after(excess)),
            jnp.where(first, 0.0, before(excess)),
        ]
        around = [own + 0.5 * e for e in around]
        diagonal[i] = DIAGONAL_SHIFT + (
            ((around[0] + around[1]) + (around[2] + around[3])) + (around[4] + around[5])
        )
        around[4] = jnp.where(last, 0.0, around[4])
        around[5] = jnp.where(first, 0.0, around[5])
        for at in range(6):
            weights[i, at] = around[at]
        second, third = coef[i, 2], stress_k[i]
        forcing = (
            0.5 * (coef[i + 1, 1] - coef[i - 1, 1]),
            0.5 * (up(second) - down(second)),
            0.5 * (jnp.where(last, 0.0, after(third)) - jnp.where(first, 0.0, before(third))),
        )
        for c in range(3):
            residual[i, c] = forcing[c]
            dir_a[i, c, 0:nj, :] = (forcing[c] * (1.0 / CENTRE))[0:nj]

    run(prepare, STEPS, writer(coef, 2, (0, 1), (0, 2)))
    send_i(STEPS + 1, reader(dir_a, 3))
    send_j(STEPS + 1, reader(dir_a, 3))

    pair = (dir_a, dir_b)
    for turn, (keep, gain) in enumerate(ratios()):
        src, dst = pair[turn % 2], pair[(turn + 1) % 2]

        def iterate(i, src=src, dst=dst, turn=turn, keep=keep, gain=gain):
            for c in range(3):
                v = src[i, c]
                applied = diagonal[i] * v - weights[i, 0] * src[i + 1, c]
                applied = applied - weights[i, 1] * src[i - 1, c]
                applied = applied - weights[i, 2] * up(v) - weights[i, 3] * down(v)
                applied = applied - weights[i, 4] * after(v) - weights[i, 5] * before(v)
                left = residual[i, c] - applied
                so_far = v if turn == 0 else total[i, c] + v
                fresh = keep * v + gain * left
                if turn < ITERS - 1:
                    residual[i, c] = left
                    total[i, c] = so_far
                    dst[i, c, 0:nj, :] = fresh[0:nj]
                else:
                    flat[c, i - 1] = (so_far + fresh)[0:nj]

        stage = STEPS + 1 + turn
        run(iterate, stage, writer(src, 3))
        if turn < ITERS - 1:
            send_i(stage + 1, reader(dst, 3))
            send_j(stage + 1, reader(dst, 3))

    moved[...] = flat[...]
    for stage in range(STEPS + 1 + ITERS):
        for way in range(4):

            @pl.when(targets[way][0])
            def _(stage=stage, way=way):
                copy(stage, way).wait_send()


def shards(mesh, phases, mobility, active, variants):
    np_, ni, nj, nk = phases.shape
    ns, nl = mesh.shape["space"], mesh.shape["slab"]
    jp = -(-(nj + 2) // 8) * 8
    flags = jnp.transpose(active[0, 0].astype(jnp.float32), (1, 0))
    speeds = mobility[:, None] * jnp.repeat(flags, nk // flags.shape[1], axis=1)
    vmem = pl.BlockSpec(memory_space=pltpu.VMEM)
    f32 = jnp.float32
    stages = STEPS + 1 + ITERS

    def scratch(*shape):
        return pltpu.VMEM(shape, f32)

    fields, solved = pl.pallas_call(
        functools.partial(kernel, (ns, nl, np_, ni, nj, nk, jp)),
        out_shape=(
            jax.ShapeDtypeStruct(phases.shape, f32),
            jax.ShapeDtypeStruct((3, ni, nj, nk), f32),
        ),
        in_specs=[vmem, vmem, pl.BlockSpec(memory_space=pltpu.SMEM)],
        out_specs=(vmem, vmem),
        scratch_shapes=[
            scratch(ni + 2, np_, jp, nk),
            scratch(ni + 2, np_, jp, nk),
            scratch(ni + 2, 3, jp, nk),
            scratch(ni + 2, jp, nk),
            scratch(ni + 2, 6, jp, nk),
            scratch(ni + 2, jp, nk),
            scratch(ni + 2, 3, jp, nk),
            scratch(ni + 2, 3, jp, nk),
            scratch(ni + 2, 3, jp, nk),
            scratch(ni + 2, 3, jp, nk),
            scratch(3, ni, nj, nk),
            scratch(STEPS, 2, np_ * nj, nk),
            scratch(STEPS, 2, np_ * nj, nk),
            scratch(STEPS, 2, ni, np_, nk),
            scratch(STEPS, 2, ni, np_, nk),
            scratch(2, 2 * nj, nk),
            scratch(2, 2 * nj, nk),
            scratch(2, ni, 2, nk),
            scratch(2, ni, 2, nk),
            scratch(ITERS, 2, 3 * nj, nk),
            scratch(ITERS, 2, 3 * nj, nk),
            scratch(ITERS, 2, ni, 3, nk),
            scratch(ITERS, 2, ni, 3, nk),
            pltpu.SemaphoreType.DMA((stages, 4)),
            pltpu.SemaphoreType.DMA((stages, 4)),
        ],
        compiler_params=pltpu.CompilerParams(
            collective_id=0, has_side_effects=True, vmem_limit_bytes=48 * 1024 * 1024
        ),
    )(phases, speeds, variants)
    arrived = lax.all_to_all(solved, "space", split_axis=3, concat_axis=1, tiled=True)
    return fields, jnp.transpose(arrived, (0, 3, 2, 1))


def solution(mesh):
    placed = (P(None, "space", "slab", None), P(), P("space", "slab", None, None), P())
    return jax.shard_map(
        functools.partial(shards, mesh),
        mesh=mesh,
        in_specs=placed,
        out_specs=(P(None, "space", "slab", None), P(None, "space", "slab", None)),
        check_vma=False,
    )
```

```python
import functools

import jax
import jax.numpy as jnp
from jax import lax
from jax.experimental import pallas as pl
from jax.experimental.pallas import tpu as pltpu
from jax.sharding import PartitionSpec as P

STEPS = 3
ITERS = 4
PAIR_ENERGY = 1.5
DIAGONAL_SHIFT = 3.0
CENTRE = 12.0
RADIUS = 9.0


def ratios():
    now = RADIUS / CENTRE
    out = []
    for _ in range(ITERS):
        later = 1.0 / (2.0 * CENTRE / RADIUS - now)
        out.append((later * now, 2.0 * later / RADIUS))
        now = later
    return out


def kernel(
    sizes,
    phases,
    speeds,
    variants,
    evolved,
    moved,
    field_a,
    field_b,
    coef,
    stress_k,
    weights,
    diagonal,
    dir_a,
    dir_b,
    residual,
    total,
    flat,
    lines,
    leaving,
    arrived,
    fsi,
    fri,
    fsj,
    frj,
    csi,
    cri,
    csj,
    crj,
    dsi,
    dri,
    dsj,
    drj,
    send_sem,
    recv_sem,
    out_sem,
    in_sem,
):
    ns, nl, np_, ni, nj, nk, jp = sizes
    space, slab = lax.axis_index("space"), lax.axis_index("slab")
    targets = (
        (space < ns - 1, {"space": jnp.minimum(space + 1, ns - 1)}),
        (space > 0, {"space": jnp.maximum(space - 1, 0)}),
        (slab < nl - 1, {"slab": jnp.minimum(slab + 1, nl - 1)}),
        (slab > 0, {"slab": jnp.maximum(slab - 1, 0)}),
    )
    mesh_id = pl.DeviceIdType.MESH
    barrier = pltpu.get_barrier_semaphore()

    def greet(o, _):
        peer = {"space": lax.rem(space + o, ns)}
        pl.semaphore_signal(barrier, inc=1, device_id=peer, device_id_type=mesh_id)
        return 0

    lax.fori_loop(1, ns, greet, 0)
    for has, where in targets[2:]:

        @pl.when(has)
        def _(where=where):
            pl.semaphore_signal(barrier, inc=1, device_id=where, device_id_type=mesh_id)

    peers = ns - 1 + jnp.minimum(slab, 1) + jnp.minimum(nl - 1 - slab, 1)
    pl.semaphore_wait(barrier, peers)

    def buffers(stage):
        if stage < STEPS:
            return fsi.at[stage], fri.at[stage], fsj.at[stage], frj.at[stage]
        if stage == STEPS:
            return csi, cri, csj, crj
        at = stage - STEPS - 1
        return dsi.at[at], dri.at[at], dsj.at[at], drj.at[at]

    def copy(stage, way):
        si, ri, sj, rj = buffers(stage)
        source, landing = (si, ri) if way < 2 else (sj, rj)
        return pltpu.make_async_remote_copy(
            src_ref=source.at[way % 2],
            dst_ref=landing.at[way % 2],
            send_sem=send_sem.at[stage, way],
            recv_sem=recv_sem.at[stage, way],
            device_id=targets[way][1],
            device_id_type=mesh_id,
        )

    def send_i(stage, read):
        count, si = read(0)[0], buffers(stage)[0]
        for side in (0, 1):

            @pl.when(targets[side][0])
            def _(side=side):
                plane = ni if side == 0 else 1
                for p in range(count):
                    si[side, p * nj : (p + 1) * nj, :] = read(p)[1](plane)
                copy(stage, side).start()

    def send_j(stage, read):
        count, sj = read(0)[0], buffers(stage)[2]
        for side in (0, 1):

            @pl.when(targets[2 + side][0])
            def _(side=side):
                row = nj - 1 if side == 0 else 0

                def body(i, _):
                    for p in range(count):
                        sj[side, i, p : p + 1, :] = read(p)[2](i + 1, row)
                    return 0

                lax.fori_loop(0, ni, body, 0)
                copy(stage, 2 + side).start()

    def take_i(stage, write):
        count, ri = write(0)[0], buffers(stage)[1]
        for side in (0, 1):

            @pl.when(targets[1 - side][0])
            def _(side=side):
                copy(stage, side).wait_recv()
                plane = 0 if side == 0 else ni + 1
                for p in range(count):
                    write(p)[1](plane, ri[side, p * nj : (p + 1) * nj, :])

    def take_j(stage, write):
        count, rj = write(0)[0], buffers(stage)[3]
        for side in (0, 1):

            @pl.when(targets[3 - side][0])
            def _(side=side):
                copy(stage, 2 + side).wait_recv()
                row = jp - 1 if side == 0 else nj

                def body(i, _):
                    for p in range(count):
                        write(p)[2](i + 1, row, rj[side, i, p : p + 1, :])
                    return 0

                lax.fori_loop(0, ni, body, 0)

    def reader(ref, count, slots_i=None, slots_j=None):
        def read(p):
            pi = slots_i[p] if slots_i else p
            pj = slots_j[p] if slots_j else p
            return (
                count,
                lambda plane: ref[plane, pi, 0:nj, :],
                lambda plane, row: ref[plane, pj, row : row + 1, :],
            )

        return read

    def writer(ref, count, slots_i=None, slots_j=None):
        def write(p):
            pi = slots_i[p] if slots_i else p
            pj = slots_j[p] if slots_j else p

            def whole(plane, value):
                ref[plane, pi, 0:nj, :] = value

            def line(plane, row, value):
                ref[plane, pj, row : row + 1, :] = value

            return count, whole, line

        return write

    def stage_in(i, _):
        for p in range(np_):
            field_a[i + 1, p, 0:nj, :] = phases[p, i]
        return 0

    lax.fori_loop(0, ni, stage_in, 0)
    send_i(0, reader(field_a, np_))
    send_j(0, reader(field_a, np_))
    for ref in (field_a, field_b, coef, dir_a, dir_b):
        count = ref.shape[1]
        blank = jnp.zeros((jp, nk), jnp.float32)
        for p in range(count):
            ref[0, p] = blank
            ref[ni + 1, p] = blank

        def clear(i, _, ref=ref, count=count):
            for p in range(count):
                ref[i + 1, p, nj:jp, :] = jnp.zeros((jp - nj, nk), jnp.float32)
            return 0

        lax.fori_loop(0, ni, clear, 0)

    lane = lax.broadcasted_iota(jnp.int32, (jp, nk), 1)
    first, last = lane == 0, lane == nk - 1

    def up(x):
        return pltpu.roll(x, jp - 1, 0)

    def down(x):
        return pltpu.roll(x, 1, 0)

    def after(x):
        return pltpu.roll(x, nk - 1, 1)

    def before(x):
        return pltpu.roll(x, 1, 1)

    def relax(i, src, store):
        squares = None
        for p in range(np_):
            x = src[i, p]
            squares = x * x if squares is None else squares + x * x
        scaled = 2.0 * PAIR_ENERGY * squares + 5.0
        for p in range(np_):
            x = src[i, p]
            around = src[i + 1, p] + src[i - 1, p] + up(x) + down(x)
            around = around + jnp.where(last, 0.0, after(x)) + jnp.where(first, 0.0, before(x))
            driving = x * (scaled + (1.0 - 2.0 * PAIR_ENERGY) * (x * x)) - around
            store(i, p, x - speeds[p : p + 1, :] * driving)

    def run(plane, stage, write):
        take_j(stage, write)
        lax.fori_loop(2, ni, lambda i, _: (plane(i), 0)[1], 0)
        take_i(stage, write)
        plane(1)
        plane(ni)

    pair = (field_a, field_b)
    for step in range(STEPS - 1):
        src, dst = pair[step % 2], pair[(step + 1) % 2]

        def store(i, p, value, dst=dst):
            dst[i, p, 0:nj, :] = value[0:nj]

        run(lambda i, src=src, store=store: relax(i, src, store), step, writer(src, np_))
        send_i(step + 1, reader(dst, np_))
        send_j(step + 1, reader(dst, np_))

    src = pair[(STEPS - 1) % 2]

    def finish(i):
        sums = [None] * 4

        def store(i, p, value):
            evolved[p, i - 1] = value[0:nj]
            square = value * value
            terms = [square] + [square * variants[p, c] for c in range(3)]
            for at, term in enumerate(terms):
                sums[at] = term if sums[at] is None else sums[at] + term

        relax(i, src, store)
        saturation = sums[0] / (1.0 + sums[0])
        excess = 0.5 * saturation
        common = (1.5 + saturation) * (sums[1] + sums[2] + sums[3])
        twice = 2.0 * (1.0 + excess)
        coef[i, 0, 0:nj, :] = excess[0:nj]
        coef[i, 1, 0:nj, :] = (common + twice * sums[1])[0:nj]
        coef[i, 2, 0:nj, :] = (common + twice * sums[2])[0:nj]
        stress_k[i] = common + twice * sums[3]

    run(finish, STEPS - 1, writer(src, np_))
    send_i(STEPS, reader(coef, 2, (0, 1), (0, 2)))
    send_j(STEPS, reader(coef, 2, (0, 1), (0, 2)))

    def prepare(i):
        excess = coef[i, 0]
        own = 1.0 + 0.5 * excess
        around = [
            coef[i + 1, 0],
            coef[i - 1, 0],
            up(excess),
            down(excess),
            jnp.where(last, 0.0, after(excess)),
            jnp.where(first, 0.0, before(excess)),
        ]
        around = [own + 0.5 * e for e in around]
        diagonal[i] = DIAGONAL_SHIFT + (
            ((around[0] + around[1]) + (around[2] + around[3])) + (around[4] + around[5])
        )
        around[4] = jnp.where(last, 0.0, around[4])
        around[5] = jnp.where(first, 0.0, around[5])
        for at in range(6):
            weights[i, at] = around[at]
        second, third = coef[i, 2], stress_k[i]
        forcing = (
            0.5 * (coef[i + 1, 1] - coef[i - 1, 1]),
            0.5 * (up(second) - down(second)),
            0.5 * (jnp.where(last, 0.0, after(third)) - jnp.where(first, 0.0, before(third))),
        )
        for c in range(3):
            residual[i, c] = forcing[c]
            dir_a[i, c, 0:nj, :] = (forcing[c] * (1.0 / CENTRE))[0:nj]

    run(prepare, STEPS, writer(coef, 2, (0, 1), (0, 2)))
    send_i(STEPS + 1, reader(dir_a, 3))
    send_j(STEPS + 1, reader(dir_a, 3))

    pair = (dir_a, dir_b)
    for turn, (keep, gain) in enumerate(ratios()):
        src, dst = pair[turn % 2], pair[(turn + 1) % 2]

        def iterate(i, src=src, dst=dst, turn=turn, keep=keep, gain=gain):
            for c in range(3):
                v = src[i, c]
                applied = diagonal[i] * v - weights[i, 0] * src[i + 1, c]
                applied = applied - weights[i, 1] * src[i - 1, c]
                applied = applied - weights[i, 2] * up(v) - weights[i, 3] * down(v)
                applied = applied - weights[i, 4] * after(v) - weights[i, 5] * before(v)
                left = residual[i, c] - applied
                so_far = v if turn == 0 else total[i, c] + v
                fresh = keep * v + gain * left
                if turn < ITERS - 1:
                    residual[i, c] = left
                    total[i, c] = so_far
                    dst[i, c, 0:nj, :] = fresh[0:nj]
                else:
                    flat[c, i - 1] = (so_far + fresh)[0:nj]

        stage = STEPS + 1 + turn
        run(iterate, stage, writer(src, 3))
        if turn < ITERS - 1:
            send_i(stage + 1, reader(dst, 3))
            send_j(stage + 1, reader(dst, 3))

    for c in range(3):
        for j in range(nj):
            row = (c * nj + j) * ni
            lines[row : row + ni, :] = flat[c, :, j, :]
    turned = jnp.transpose(lines[...])
    depth = nk // ns
    for d in range(ns):
        leaving[d] = turned[d * depth : (d + 1) * depth, :]

    def block(other, slot):
        return pltpu.make_async_remote_copy(
            src_ref=leaving.at[other],
            dst_ref=arrived.at[slot],
            send_sem=out_sem.at[other],
            recv_sem=in_sem.at[slot],
            device_id={"space": other},
            device_id_type=mesh_id,
        )

    lax.fori_loop(1, ns, lambda o, _: (block(lax.rem(space + o, ns), space).start(), 0)[1], 0)
    arrived[space] = leaving[space]

    def landed(o, _):
        other = lax.rem(space + o, ns)
        block(other, other).wait_recv()
        return 0

    lax.fori_loop(1, ns, landed, 0)
    for c in range(3):
        for j in range(nj):
            at = (c * nj + j) * ni
            parts = [arrived[d, :, at : at + ni] for d in range(ns)]
            moved[c, :, j, :] = jnp.concatenate(parts, axis=1)
    lax.fori_loop(
        1, ns, lambda o, _: (block(lax.rem(space + o, ns), space).wait_send(), 0)[1], 0
    )
    for stage in range(STEPS + 1 + ITERS):
        for way in range(4):

            @pl.when(targets[way][0])
            def _(stage=stage, way=way):
                copy(stage, way).wait_send()


def shards(mesh, phases, mobility, active, variants):
    np_, ni, nj, nk = phases.shape
    ns, nl = mesh.shape["space"], mesh.shape["slab"]
    jp = -(-(nj + 2) // 8) * 8
    flags = jnp.transpose(active[0, 0].astype(jnp.float32), (1, 0))
    speeds = mobility[:, None] * jnp.repeat(flags, nk // flags.shape[1], axis=1)
    vmem = pl.BlockSpec(memory_space=pltpu.VMEM)
    f32 = jnp.float32
    stages = STEPS + 1 + ITERS

    def scratch(*shape):
        return pltpu.VMEM(shape, f32)

    return pl.pallas_call(
        functools.partial(kernel, (ns, nl, np_, ni, nj, nk, jp)),
        out_shape=(
            jax.ShapeDtypeStruct(phases.shape, f32),
            jax.ShapeDtypeStruct((3, nk // ns, nj, ni * ns), f32),
        ),
        in_specs=[vmem, vmem, pl.BlockSpec(memory_space=pltpu.SMEM)],
        out_specs=(vmem, vmem),
        scratch_shapes=[
            scratch(ni + 2, np_, jp, nk),
            scratch(ni + 2, np_, jp, nk),
            scratch(ni + 2, 3, jp, nk),
            scratch(ni + 2, jp, nk),
            scratch(ni + 2, 6, jp, nk),
            scratch(ni + 2, jp, nk),
            scratch(ni + 2, 3, jp, nk),
            scratch(ni + 2, 3, jp, nk),
            scratch(ni + 2, 3, jp, nk),
            scratch(ni + 2, 3, jp, nk),
            scratch(3, ni, nj, nk),
            scratch(3 * ni * nj, nk),
            scratch(ns, nk // ns, 3 * ni * nj),
            scratch(ns, nk // ns, 3 * ni * nj),
            scratch(STEPS, 2, np_ * nj, nk),
            scratch(STEPS, 2, np_ * nj, nk),
            scratch(STEPS, 2, ni, np_, nk),
            scratch(STEPS, 2, ni, np_, nk),
            scratch(2, 2 * nj, nk),
            scratch(2, 2 * nj, nk),
            scratch(2, ni, 2, nk),
            scratch(2, ni, 2, nk),
            scratch(ITERS, 2, 3 * nj, nk),
            scratch(ITERS, 2, 3 * nj, nk),
            scratch(ITERS, 2, ni, 3, nk),
            scratch(ITERS, 2, ni, 3, nk),
            pltpu.SemaphoreType.DMA((stages, 4)),
            pltpu.SemaphoreType.DMA((stages, 4)),
            pltpu.SemaphoreType.DMA((ns,)),
            pltpu.SemaphoreType.DMA((ns,)),
        ],
        compiler_params=pltpu.CompilerParams(
            collective_id=0, has_side_effects=True, vmem_limit_bytes=48 * 1024 * 1024
        ),
    )(phases, speeds, variants)


def solution(mesh):
    placed = (P(None, "space", "slab", None), P(), P("space", "slab", None, None), P())
    return jax.shard_map(
        functools.partial(shards, mesh),
        mesh=mesh,
        in_specs=placed,
        out_specs=(P(None, "space", "slab", None), P(None, "space", "slab", None)),
        check_vma=False,
    )
```

```python
import functools

import jax
import jax.numpy as jnp
from jax import lax
from jax.experimental import pallas as pl
from jax.experimental.pallas import tpu as pltpu
from jax.sharding import PartitionSpec as P

STEPS = 3
ITERS = 4
PAIR_ENERGY = 1.5
DIAGONAL_SHIFT = 3.0
CENTRE = 12.0
RADIUS = 9.0


def ratios():
    now = RADIUS / CENTRE
    out = []
    for _ in range(ITERS):
        later = 1.0 / (2.0 * CENTRE / RADIUS - now)
        out.append((later * now, 2.0 * later / RADIUS))
        now = later
    return out


def kernel(
    sizes,
    phases,
    mobility,
    active,
    variants,
    evolved,
    moved,
    speeds,
    field_a,
    field_b,
    field_c,
    sums,
    coef,
    stress_k,
    weights,
    diagonal,
    dir_a,
    dir_b,
    residual,
    total,
    flat,
    lines,
    leaving,
    arrived,
    csi,
    cri,
    csj,
    crj,
    dsi,
    dri,
    dsj,
    drj,
    send_sem,
    recv_sem,
    out_sem,
    in_sem,
):
    ns, nl, np_, ni, nj, nk, jp = sizes
    space, slab = lax.axis_index("space"), lax.axis_index("slab")
    targets = (
        (space < ns - 1, {"space": jnp.minimum(space + 1, ns - 1)}),
        (space > 0, {"space": jnp.maximum(space - 1, 0)}),
        (slab < nl - 1, {"slab": jnp.minimum(slab + 1, nl - 1)}),
        (slab > 0, {"slab": jnp.maximum(slab - 1, 0)}),
    )
    mesh_id = pl.DeviceIdType.MESH
    barrier = pltpu.get_barrier_semaphore()

    def greet(o, _):
        peer = {"space": lax.rem(space + o, ns)}
        pl.semaphore_signal(barrier, inc=1, device_id=peer, device_id_type=mesh_id)
        return 0

    lax.fori_loop(1, ns, greet, 0)
    for has, where in targets[2:]:

        @pl.when(has)
        def _(where=where):
            pl.semaphore_signal(barrier, inc=1, device_id=where, device_id_type=mesh_id)

    peers = ns - 1 + jnp.minimum(slab, 1) + jnp.minimum(nl - 1 - slab, 1)
    pl.semaphore_wait(barrier, peers)

    def buffers(stage):
        if stage == STEPS:
            return csi, cri, csj, crj
        at = stage - STEPS - 1
        return dsi.at[at], dri.at[at], dsj.at[at], drj.at[at]

    def copy(stage, way):
        si, ri, sj, rj = buffers(stage)
        source, landing = (si, ri) if way < 2 else (sj, rj)
        return pltpu.make_async_remote_copy(
            src_ref=source.at[way % 2],
            dst_ref=landing.at[way % 2],
            send_sem=send_sem.at[stage, way],
            recv_sem=recv_sem.at[stage, way],
            device_id=targets[way][1],
            device_id_type=mesh_id,
        )

    fields = (field_a, field_b, field_c)

    def face(stage, way):
        ref, mid_i, mid_j = fields[stage], pl.ds(1, ni), pl.ds(1, nj)
        source, landing = (
            ((ni, mid_j), (0, mid_j)),
            ((1, mid_j), (ni + 1, mid_j)),
            ((mid_i, nj), (mid_i, 0)),
            ((mid_i, 1), (mid_i, nj + 1)),
        )[way]
        return pltpu.make_async_remote_copy(
            src_ref=ref.at[source],
            dst_ref=ref.at[landing],
            send_sem=send_sem.at[stage, way],
            recv_sem=recv_sem.at[stage, way],
            device_id=targets[way][1],
            device_id_type=mesh_id,
        )

    def send_face(stage, way):
        pl.when(targets[way][0])(lambda: face(stage, way).start())

    def take_face(stage, way):
        pl.when(targets[way ^ 1][0])(lambda: face(stage, way).wait_recv())

    def send_i(stage, read):
        count, si = read(0)[0], buffers(stage)[0]
        for side in (0, 1):

            @pl.when(targets[side][0])
            def _(side=side):
                plane = ni if side == 0 else 1
                for p in range(count):
                    si[side, p * nj : (p + 1) * nj, :] = read(p)[1](plane)
                copy(stage, side).start()

    def send_j(stage, read):
        count, sj = read(0)[0], buffers(stage)[2]
        for side in (0, 1):

            @pl.when(targets[2 + side][0])
            def _(side=side):
                row = nj - 1 if side == 0 else 0

                def body(i, _):
                    for p in range(count):
                        sj[side, i, p : p + 1, :] = read(p)[2](i + 1, row)
                    return 0

                lax.fori_loop(0, ni, body, 0)
                copy(stage, 2 + side).start()

    def take_i(stage, write):
        count, ri = write(0)[0], buffers(stage)[1]
        for side in (0, 1):

            @pl.when(targets[1 - side][0])
            def _(side=side):
                copy(stage, side).wait_recv()
                plane = 0 if side == 0 else ni + 1
                for p in range(count):
                    write(p)[1](plane, ri[side, p * nj : (p + 1) * nj, :])

    def take_j(stage, write):
        count, rj = write(0)[0], buffers(stage)[3]
        for side in (0, 1):

            @pl.when(targets[3 - side][0])
            def _(side=side):
                copy(stage, 2 + side).wait_recv()
                row = jp - 1 if side == 0 else nj

                def body(i, _):
                    for p in range(count):
                        write(p)[2](i + 1, row, rj[side, i, p : p + 1, :])
                    return 0

                lax.fori_loop(0, ni, body, 0)

    def reader(ref, count, slots_i=None, slots_j=None):
        def read(p):
            pi = slots_i[p] if slots_i else p
            pj = slots_j[p] if slots_j else p
            return (
                count,
                lambda plane: ref[plane, pi, 0:nj, :],
                lambda plane, row: ref[plane, pj, row : row + 1, :],
            )

        return read

    def writer(ref, count, slots_i=None, slots_j=None):
        def write(p):
            pi = slots_i[p] if slots_i else p
            pj = slots_j[p] if slots_j else p

            def whole(plane, value):
                ref[plane, pi, 0:nj, :] = value

            def line(plane, row, value):
                ref[plane, pj, row : row + 1, :] = value

            return count, whole, line

        return write

    def stage_in(i):
        for j in range(nj):
            field_a[i, j + 1] = phases[i - 1, j]

    stage_in(1)
    send_face(0, 1)
    stage_in(ni)
    send_face(0, 0)
    lax.fori_loop(2, ni, lambda i, _: (stage_in(i), 0)[1], 0)
    send_face(0, 2)
    send_face(0, 3)

    def wipe(way, plane):
        @pl.when(jnp.logical_not(targets[way][0]))
        def _():
            for ref in fields:
                if way < 2:
                    for j in range(nj):
                        ref[plane, j + 1] = jnp.zeros((np_, nk), jnp.float32)
                else:
                    for i in range(ni):
                        ref[i + 1, plane] = jnp.zeros((np_, nk), jnp.float32)

    wipe(0, ni + 1)
    wipe(1, 0)
    wipe(2, nj + 1)
    wipe(3, 0)
    bricks = active.shape[0]
    owner = lax.broadcasted_iota(jnp.int32, (bricks, nk), 1) // (nk // bricks)
    spread = (owner == lax.broadcasted_iota(jnp.int32, (bricks, nk), 0)).astype(jnp.float32)
    speeds[...] = lax.dot_general(
        active[...].astype(jnp.float32) * mobility[...],
        spread,
        (((0,), (0,)), ((), ())),
        precision=lax.Precision.HIGHEST,
        preferred_element_type=jnp.float32,
    )
    for ref in (coef, dir_a, dir_b):
        count = ref.shape[1]
        blank = jnp.zeros((jp, nk), jnp.float32)
        for p in range(count):
            ref[0, p] = blank
            ref[ni + 1, p] = blank

        def clear(i, _, ref=ref, count=count):
            for p in range(count):
                ref[i + 1, p, nj:jp, :] = jnp.zeros((jp - nj, nk), jnp.float32)
            return 0

        lax.fori_loop(0, ni, clear, 0)

    lane = lax.broadcasted_iota(jnp.int32, (jp, nk), 1)
    first, last = lane == 0, lane == nk - 1

    def up(x):
        return pltpu.roll(x, jp - 1, 0)

    def down(x):
        return pltpu.roll(x, 1, 0)

    def after(x):
        return pltpu.roll(x, nk - 1, 1)

    def before(x):
        return pltpu.roll(x, 1, 1)

    lane_8 = lax.broadcasted_iota(jnp.int32, (np_, nk), 1)
    first_8, last_8 = lane_8 == 0, lane_8 == nk - 1

    def relax(i, j, src, store):
        x = src[i, j]
        square = x * x
        squares = jnp.sum(square, axis=0, keepdims=True)
        scaled = 2.0 * PAIR_ENERGY * squares + 5.0
        around = (src[i + 1, j] + src[i - 1, j]) + (src[i, j + 1] + src[i, j - 1])
        around = around + jnp.where(last_8, 0.0, after(x)) + jnp.where(first_8, 0.0, before(x))
        driving = x * (scaled + (1.0 - 2.0 * PAIR_ENERGY) * square) - around
        store(i, j, x - speeds[...] * driving)

    def advance(stage, store):
        src = fields[stage]

        def rows(i, columns):
            for j in columns:
                relax(i, j, src, store)

        lax.fori_loop(2, ni, lambda i, _: (rows(i, range(2, nj)), 0)[1], 0)
        take_face(stage, 2)
        take_face(stage, 3)
        lax.fori_loop(2, ni, lambda i, _: (rows(i, (1, nj)), 0)[1], 0)
        take_face(stage, 0)
        rows(1, range(1, nj + 1))
        if stage < STEPS - 1:
            send_face(stage + 1, 1)
        take_face(stage, 1)
        rows(ni, range(1, nj + 1))
        if stage < STEPS - 1:
            send_face(stage + 1, 0)
            send_face(stage + 1, 2)
            send_face(stage + 1, 3)

    def run(plane, stage, write):
        take_j(stage, write)
        lax.fori_loop(2, ni, lambda i, _: (plane(i), 0)[1], 0)
        take_i(stage, write)
        plane(1)
        plane(ni)

    for step in range(STEPS - 1):

        def store(i, j, value, dst=fields[step + 1]):
            dst[i, j] = value

        advance(step, store)

    def finish(i, j, value):
        evolved[i - 1, j - 1] = value
        square = value * value
        sums[i, 0, j - 1 : j, :] = jnp.sum(square, axis=0, keepdims=True)
        for c in range(3):
            scaled = square * variants[:, c : c + 1]
            sums[i, c + 1, j - 1 : j, :] = jnp.sum(scaled, axis=0, keepdims=True)

    advance(STEPS - 1, finish)

    def derive(i):
        sum_0, sum_1, sum_2, sum_3 = (sums[i, at] for at in range(4))
        saturation = sum_0 / (1.0 + sum_0)
        excess = 0.5 * saturation
        common = (1.5 + saturation) * (sum_1 + sum_2 + sum_3)
        twice = 2.0 * (1.0 + excess)
        coef[i, 0, 0:nj, :] = excess[0:nj]
        coef[i, 1, 0:nj, :] = (common + twice * sum_1)[0:nj]
        coef[i, 2, 0:nj, :] = (common + twice * sum_2)[0:nj]
        stress_k[i] = common + twice * sum_3

    lax.fori_loop(1, ni + 1, lambda i, _: (derive(i), 0)[1], 0)
    send_i(STEPS, reader(coef, 2, (0, 1), (0, 2)))
    send_j(STEPS, reader(coef, 2, (0, 1), (0, 2)))

    def prepare(i):
        excess = coef[i, 0]
        own = 1.0 + 0.5 * excess
        around = [
            coef[i + 1, 0],
            coef[i - 1, 0],
            up(excess),
            down(excess),
            jnp.where(last, 0.0, after(excess)),
            jnp.where(first, 0.0, before(excess)),
        ]
        around = [own + 0.5 * e for e in around]
        diagonal[i] = DIAGONAL_SHIFT + (
            ((around[0] + around[1]) + (around[2] + around[3])) + (around[4] + around[5])
        )
        around[4] = jnp.where(last, 0.0, around[4])
        around[5] = jnp.where(first, 0.0, around[5])
        for at in range(6):
            weights[i, at] = around[at]
        second, third = coef[i, 2], stress_k[i]
        forcing = (
            0.5 * (coef[i + 1, 1] - coef[i - 1, 1]),
            0.5 * (up(second) - down(second)),
            0.5 * (jnp.where(last, 0.0, after(third)) - jnp.where(first, 0.0, before(third))),
        )
        for c in range(3):
            residual[i, c] = forcing[c]
            dir_a[i, c, 0:nj, :] = (forcing[c] * (1.0 / CENTRE))[0:nj]

    run(prepare, STEPS, writer(coef, 2, (0, 1), (0, 2)))
    send_i(STEPS + 1, reader(dir_a, 3))
    send_j(STEPS + 1, reader(dir_a, 3))

    pair = (dir_a, dir_b)
    for turn, (keep, gain) in enumerate(ratios()):
        src, dst = pair[turn % 2], pair[(turn + 1) % 2]

        def iterate(i, src=src, dst=dst, turn=turn, keep=keep, gain=gain):
            for c in range(3):
                v = src[i, c]
                applied = diagonal[i] * v - weights[i, 0] * src[i + 1, c]
                applied = applied - weights[i, 1] * src[i - 1, c]
                applied = applied - weights[i, 2] * up(v) - weights[i, 3] * down(v)
                applied = applied - weights[i, 4] * after(v) - weights[i, 5] * before(v)
                left = residual[i, c] - applied
                so_far = v if turn == 0 else total[i, c] + v
                fresh = keep * v + gain * left
                if turn < ITERS - 1:
                    residual[i, c] = left
                    total[i, c] = so_far
                    dst[i, c, 0:nj, :] = fresh[0:nj]
                else:
                    flat[c, i - 1] = (so_far + fresh)[0:nj]

        stage = STEPS + 1 + turn
        run(iterate, stage, writer(src, 3))
        if turn < ITERS - 1:
            send_i(stage + 1, reader(dst, 3))
            send_j(stage + 1, reader(dst, 3))

    for c in range(3):
        for j in range(nj):
            row = (c * nj + j) * ni
            lines[row : row + ni, :] = flat[c, :, j, :]
    turned = jnp.transpose(lines[...])
    depth = nk // ns
    for d in range(ns):
        leaving[d] = turned[d * depth : (d + 1) * depth, :]

    def block(other, slot):
        return pltpu.make_async_remote_copy(
            src_ref=leaving.at[other],
            dst_ref=arrived.at[slot],
            send_sem=out_sem.at[other],
            recv_sem=in_sem.at[slot],
            device_id={"space": other},
            device_id_type=mesh_id,
        )

    lax.fori_loop(1, ns, lambda o, _: (block(lax.rem(space + o, ns), space).start(), 0)[1], 0)
    arrived[space] = leaving[space]

    def landed(o, _):
        other = lax.rem(space + o, ns)
        block(other, other).wait_recv()
        return 0

    lax.fori_loop(1, ns, landed, 0)
    for c in range(3):
        for j in range(nj):
            at = (c * nj + j) * ni
            parts = [arrived[d, :, at : at + ni] for d in range(ns)]
            moved[c, j] = jnp.concatenate(parts, axis=1)
    lax.fori_loop(
        1, ns, lambda o, _: (block(lax.rem(space + o, ns), space).wait_send(), 0)[1], 0
    )
    for stage in range(STEPS + 1 + ITERS):
        for way in range(4):

            @pl.when(targets[way][0])
            def _(stage=stage, way=way):
                (face if stage < STEPS else copy)(stage, way).wait_send()


def shards(mesh, phases, mobility, active, variants):
    np_, ni, nj, nk = phases.shape
    ns, nl = mesh.shape["space"], mesh.shape["slab"]
    jp = -(-(nj + 2) // 8) * 8
    vmem = pl.BlockSpec(memory_space=pltpu.VMEM)
    f32 = jnp.float32
    stages = STEPS + 1 + ITERS

    def scratch(*shape):
        return pltpu.VMEM(shape, f32)

    fields, moved = pl.pallas_call(
        functools.partial(kernel, (ns, nl, np_, ni, nj, nk, jp)),
        out_shape=(
            jax.ShapeDtypeStruct((ni, nj, np_, nk), f32),
            jax.ShapeDtypeStruct((3, nj, nk // ns, ni * ns), f32),
        ),
        in_specs=[vmem, vmem, vmem, vmem],
        out_specs=(vmem, vmem),
        scratch_shapes=[
            scratch(np_, nk),
            scratch(ni + 2, nj + 2, np_, nk),
            scratch(ni + 2, nj + 2, np_, nk),
            scratch(ni + 2, nj + 2, np_, nk),
            scratch(ni + 2, 4, jp, nk),
            scratch(ni + 2, 3, jp, nk),
            scratch(ni + 2, jp, nk),
            scratch(ni + 2, 6, jp, nk),
            scratch(ni + 2, jp, nk),
            scratch(ni + 2, 3, jp, nk),
            scratch(ni + 2, 3, jp, nk),
            scratch(ni + 2, 3, jp, nk),
            scratch(ni + 2, 3, jp, nk),
            scratch(3, ni, nj, nk),
            scratch(3 * ni * nj, nk),
            scratch(ns, nk // ns, 3 * ni * nj),
            scratch(ns, nk // ns, 3 * ni * nj),
            scratch(2, 2 * nj, nk),
            scratch(2, 2 * nj, nk),
            scratch(2, ni, 2, nk),
            scratch(2, ni, 2, nk),
            scratch(ITERS, 2, 3 * nj, nk),
            scratch(ITERS, 2, 3 * nj, nk),
            scratch(ITERS, 2, ni, 3, nk),
            scratch(ITERS, 2, ni, 3, nk),
            pltpu.SemaphoreType.DMA((stages, 4)),
            pltpu.SemaphoreType.DMA((stages, 4)),
            pltpu.SemaphoreType.DMA((ns,)),
            pltpu.SemaphoreType.DMA((ns,)),
        ],
        compiler_params=pltpu.CompilerParams(
            collective_id=0, has_side_effects=True, vmem_limit_bytes=48 * 1024 * 1024
        ),
    )(jnp.transpose(phases, (1, 2, 0, 3)), mobility[None], active[0, 0], variants)
    return jnp.transpose(fields, (2, 0, 1, 3)), jnp.transpose(moved, (0, 2, 1, 3))


def solution(mesh):
    placed = (P(None, "space", "slab", None), P(), P("space", "slab", None, None), P())
    return jax.shard_map(
        functools.partial(shards, mesh),
        mesh=mesh,
        in_specs=placed,
        out_specs=(P(None, "space", "slab", None), P(None, "space", "slab", None)),
        check_vma=False,
    )
```

```python
import functools

import jax
import jax.numpy as jnp
from jax import lax
from jax.experimental import pallas as pl
from jax.experimental.pallas import tpu as pltpu
from jax.sharding import PartitionSpec as P

STEPS = 3
ITERS = 4
PAIR_ENERGY = 1.5
DIAGONAL_SHIFT = 3.0
CENTRE = 12.0
RADIUS = 9.0


def ratios():
    now = RADIUS / CENTRE
    out = []
    for _ in range(ITERS):
        later = 1.0 / (2.0 * CENTRE / RADIUS - now)
        out.append((later * now, 2.0 * later / RADIUS))
        now = later
    return out


def kernel(
    sizes,
    phases,
    speeds,
    variants,
    evolved,
    moved,
    field_a,
    field_b,
    coef,
    stress_k,
    weights,
    diagonal,
    dir_a,
    dir_b,
    residual,
    total,
    flat,
    lines,
    leaving,
    arrived,
    fsi,
    fri,
    fsj,
    frj,
    csi,
    cri,
    csj,
    crj,
    dsi,
    dri,
    dsj,
    drj,
    send_sem,
    recv_sem,
    out_sem,
    in_sem,
):
    ns, nl, np_, ni, nj, nk, jp = sizes
    space, slab = lax.axis_index("space"), lax.axis_index("slab")
    targets = (
        (space < ns - 1, {"space": jnp.minimum(space + 1, ns - 1)}),
        (space > 0, {"space": jnp.maximum(space - 1, 0)}),
        (slab < nl - 1, {"slab": jnp.minimum(slab + 1, nl - 1)}),
        (slab > 0, {"slab": jnp.maximum(slab - 1, 0)}),
    )
    mesh_id = pl.DeviceIdType.MESH
    barrier = pltpu.get_barrier_semaphore()

    def greet(o, _):
        peer = {"space": lax.rem(space + o, ns)}
        pl.semaphore_signal(barrier, inc=1, device_id=peer, device_id_type=mesh_id)
        return 0

    lax.fori_loop(1, ns, greet, 0)
    for has, where in targets[2:]:

        @pl.when(has)
        def _(where=where):
            pl.semaphore_signal(barrier, inc=1, device_id=where, device_id_type=mesh_id)

    peers = ns - 1 + jnp.minimum(slab, 1) + jnp.minimum(nl - 1 - slab, 1)
    pl.semaphore_wait(barrier, peers)

    def buffers(stage):
        if stage < STEPS:
            return fsi.at[stage], fri.at[stage], fsj.at[stage], frj.at[stage]
        if stage == STEPS:
            return csi, cri, csj, crj
        at = stage - STEPS - 1
        return dsi.at[at], dri.at[at], dsj.at[at], drj.at[at]

    def copy(stage, way):
        si, ri, sj, rj = buffers(stage)
        source, landing = (si, ri) if way < 2 else (sj, rj)
        return pltpu.make_async_remote_copy(
            src_ref=source.at[way % 2],
            dst_ref=landing.at[way % 2],
            send_sem=send_sem.at[stage, way],
            recv_sem=recv_sem.at[stage, way],
            device_id=targets[way][1],
            device_id_type=mesh_id,
        )

    def send_i(stage, read):
        count, si = read(0)[0], buffers(stage)[0]
        for side in (0, 1):

            @pl.when(targets[side][0])
            def _(side=side):
                plane = ni if side == 0 else 1
                for p in range(count):
                    si[side, p * nj : (p + 1) * nj, :] = read(p)[1](plane)
                copy(stage, side).start()

    def send_j(stage, read):
        count, sj = read(0)[0], buffers(stage)[2]
        for side in (0, 1):

            @pl.when(targets[2 + side][0])
            def _(side=side):
                row = nj - 1 if side == 0 else 0

                def body(i, _):
                    for p in range(count):
                        sj[side, i, p : p + 1, :] = read(p)[2](i + 1, row)
                    return 0

                lax.fori_loop(0, ni, body, 0)
                copy(stage, 2 + side).start()

    def take_i(stage, write):
        count, ri = write(0)[0], buffers(stage)[1]
        for side in (0, 1):

            @pl.when(targets[1 - side][0])
            def _(side=side):
                copy(stage, side).wait_recv()
                plane = 0 if side == 0 else ni + 1
                for p in range(count):
                    write(p)[1](plane, ri[side, p * nj : (p + 1) * nj, :])

    def take_j(stage, write):
        count, rj = write(0)[0], buffers(stage)[3]
        for side in (0, 1):

            @pl.when(targets[3 - side][0])
            def _(side=side):
                copy(stage, 2 + side).wait_recv()
                row = jp - 1 if side == 0 else nj

                def body(i, _):
                    for p in range(count):
                        write(p)[2](i + 1, row, rj[side, i, p : p + 1, :])
                    return 0

                lax.fori_loop(0, ni, body, 0)

    def reader(ref, count, slots_i=None, slots_j=None):
        def read(p):
            pi = slots_i[p] if slots_i else p
            pj = slots_j[p] if slots_j else p
            return (
                count,
                lambda plane: ref[plane, pi, 0:nj, :],
                lambda plane, row: ref[plane, pj, row : row + 1, :],
            )

        return read

    def writer(ref, count, slots_i=None, slots_j=None):
        def write(p):
            pi = slots_i[p] if slots_i else p
            pj = slots_j[p] if slots_j else p

            def whole(plane, value):
                ref[plane, pi, 0:nj, :] = value

            def line(plane, row, value):
                ref[plane, pj, row : row + 1, :] = value

            return count, whole, line

        return write

    def stage_in(i, _):
        for p in range(np_):
            field_a[i + 1, p, 0:nj, :] = phases[p, i]
        return 0

    lax.fori_loop(0, ni, stage_in, 0)
    send_i(0, reader(field_a, np_))
    send_j(0, reader(field_a, np_))
    for ref in (field_a, field_b, coef, dir_a, dir_b):
        count = ref.shape[1]
        blank = jnp.zeros((jp, nk), jnp.float32)
        for p in range(count):
            ref[0, p] = blank
            ref[ni + 1, p] = blank

        def clear(i, _, ref=ref, count=count):
            for p in range(count):
                ref[i + 1, p, nj:jp, :] = jnp.zeros((jp - nj, nk), jnp.float32)
            return 0

        lax.fori_loop(0, ni, clear, 0)

    lane = lax.broadcasted_iota(jnp.int32, (jp, nk), 1)
    first, last = lane == 0, lane == nk - 1

    def up(x):
        return pltpu.roll(x, jp - 1, 0)

    def down(x):
        return pltpu.roll(x, 1, 0)

    def after(x):
        return pltpu.roll(x, nk - 1, 1)

    def before(x):
        return pltpu.roll(x, 1, 1)

    def relax(i, src, store):
        squares = None
        for p in range(np_):
            x = src[i, p]
            squares = x * x if squares is None else squares + x * x
        scaled = 2.0 * PAIR_ENERGY * squares + 5.0
        for p in range(np_):
            x = src[i, p]
            around = src[i + 1, p] + src[i - 1, p] + up(x) + down(x)
            around = around + jnp.where(last, 0.0, after(x)) + jnp.where(first, 0.0, before(x))
            driving = x * (scaled + (1.0 - 2.0 * PAIR_ENERGY) * (x * x)) - around
            store(i, p, x - speeds[p : p + 1, :] * driving)

    def run(plane, stage, write):
        take_j(stage, write)
        lax.fori_loop(2, ni, lambda i, _: (plane(i), 0)[1], 0)
        take_i(stage, write)
        plane(1)
        plane(ni)

    pair = (field_a, field_b)
    for step in range(STEPS - 1):
        src, dst = pair[step % 2], pair[(step + 1) % 2]

        def store(i, p, value, dst=dst):
            dst[i, p, 0:nj, :] = value[0:nj]

        run(lambda i, src=src, store=store: relax(i, src, store), step, writer(src, np_))
        send_i(step + 1, reader(dst, np_))
        send_j(step + 1, reader(dst, np_))

    src = pair[(STEPS - 1) % 2]

    def finish(i):
        sums = [None] * 4

        def store(i, p, value):
            evolved[p, i - 1] = value[0:nj]
            square = value * value
            terms = [square] + [square * variants[p, c] for c in range(3)]
            for at, term in enumerate(terms):
                sums[at] = term if sums[at] is None else sums[at] + term

        relax(i, src, store)
        saturation = sums[0] / (1.0 + sums[0])
        excess = 0.5 * saturation
        common = (1.5 + saturation) * (sums[1] + sums[2] + sums[3])
        twice = 2.0 * (1.0 + excess)
        coef[i, 0, 0:nj, :] = excess[0:nj]
        coef[i, 1, 0:nj, :] = (common + twice * sums[1])[0:nj]
        coef[i, 2, 0:nj, :] = (common + twice * sums[2])[0:nj]
        stress_k[i] = common + twice * sums[3]

    run(finish, STEPS - 1, writer(src, np_))
    send_i(STEPS, reader(coef, 2, (0, 1), (0, 2)))
    send_j(STEPS, reader(coef, 2, (0, 1), (0, 2)))

    def prepare(i):
        excess = coef[i, 0]
        own = 1.0 + 0.5 * excess
        around = [
            coef[i + 1, 0],
            coef[i - 1, 0],
            up(excess),
            down(excess),
            jnp.where(last, 0.0, after(excess)),
            jnp.where(first, 0.0, before(excess)),
        ]
        around = [own + 0.5 * e for e in around]
        diagonal[i] = DIAGONAL_SHIFT + (
            ((around[0] + around[1]) + (around[2] + around[3])) + (around[4] + around[5])
        )
        around[4] = jnp.where(last, 0.0, around[4])
        around[5] = jnp.where(first, 0.0, around[5])
        for at in range(6):
            weights[i, at] = around[at]
        second, third = coef[i, 2], stress_k[i]
        forcing = (
            0.5 * (coef[i + 1, 1] - coef[i - 1, 1]),
            0.5 * (up(second) - down(second)),
            0.5 * (jnp.where(last, 0.0, after(third)) - jnp.where(first, 0.0, before(third))),
        )
        for c in range(3):
            residual[i, c] = forcing[c]
            dir_a[i, c, 0:nj, :] = (forcing[c] * (1.0 / CENTRE))[0:nj]

    run(prepare, STEPS, writer(coef, 2, (0, 1), (0, 2)))
    send_i(STEPS + 1, reader(dir_a, 3))
    send_j(STEPS + 1, reader(dir_a, 3))

    pair = (dir_a, dir_b)
    for turn, (keep, gain) in enumerate(ratios()):
        src, dst = pair[turn % 2], pair[(turn + 1) % 2]

        def iterate(i, src=src, dst=dst, turn=turn, keep=keep, gain=gain):
            for c in range(3):
                v = src[i, c]
                applied = diagonal[i] * v - weights[i, 0] * src[i + 1, c]
                applied = applied - weights[i, 1] * src[i - 1, c]
                applied = applied - weights[i, 2] * up(v) - weights[i, 3] * down(v)
                applied = applied - weights[i, 4] * after(v) - weights[i, 5] * before(v)
                left = residual[i, c] - applied
                so_far = v if turn == 0 else total[i, c] + v
                fresh = keep * v + gain * left
                if turn < ITERS - 1:
                    residual[i, c] = left
                    total[i, c] = so_far
                    dst[i, c, 0:nj, :] = fresh[0:nj]
                else:
                    flat[c, i - 1] = (so_far + fresh)[0:nj]

        stage = STEPS + 1 + turn
        run(iterate, stage, writer(src, 3))
        if turn < ITERS - 1:
            send_i(stage + 1, reader(dst, 3))
            send_j(stage + 1, reader(dst, 3))

    for c in range(3):
        for j in range(nj):
            row = (c * nj + j) * ni
            lines[row : row + ni, :] = flat[c, :, j, :]
    turned = jnp.transpose(lines[...])
    depth = nk // ns
    for d in range(ns):
        leaving[d] = turned[d * depth : (d + 1) * depth, :]

    def block(other, slot):
        return pltpu.make_async_remote_copy(
            src_ref=leaving.at[other],
            dst_ref=arrived.at[slot],
            send_sem=out_sem.at[other],
            recv_sem=in_sem.at[slot],
            device_id={"space": other},
            device_id_type=mesh_id,
        )

    lax.fori_loop(1, ns, lambda o, _: (block(lax.rem(space + o, ns), space).start(), 0)[1], 0)
    arrived[space] = leaving[space]

    def landed(o, _):
        other = lax.rem(space + o, ns)
        block(other, other).wait_recv()
        return 0

    lax.fori_loop(1, ns, landed, 0)
    for c in range(3):
        for j in range(nj):
            at = (c * nj + j) * ni
            parts = [arrived[d, :, at : at + ni] for d in range(ns)]
            moved[c, j] = jnp.concatenate(parts, axis=1)
    lax.fori_loop(
        1, ns, lambda o, _: (block(lax.rem(space + o, ns), space).wait_send(), 0)[1], 0
    )
    for stage in range(STEPS + 1 + ITERS):
        for way in range(4):

            @pl.when(targets[way][0])
            def _(stage=stage, way=way):
                copy(stage, way).wait_send()


def shards(mesh, phases, mobility, active, variants):
    np_, ni, nj, nk = phases.shape
    ns, nl = mesh.shape["space"], mesh.shape["slab"]
    jp = -(-(nj + 2) // 8) * 8
    flags = jnp.transpose(active[0, 0].astype(jnp.float32), (1, 0))
    speeds = mobility[:, None] * jnp.repeat(flags, nk // flags.shape[1], axis=1)
    vmem = pl.BlockSpec(memory_space=pltpu.VMEM)
    f32 = jnp.float32
    stages = STEPS + 1 + ITERS

    def scratch(*shape):
        return pltpu.VMEM(shape, f32)

    fields, moved = pl.pallas_call(
        functools.partial(kernel, (ns, nl, np_, ni, nj, nk, jp)),
        out_shape=(
            jax.ShapeDtypeStruct(phases.shape, f32),
            jax.ShapeDtypeStruct((3, nj, nk // ns, ni * ns), f32),
        ),
        in_specs=[vmem, vmem, pl.BlockSpec(memory_space=pltpu.SMEM)],
        out_specs=(vmem, vmem),
        scratch_shapes=[
            scratch(ni + 2, np_, jp, nk),
            scratch(ni + 2, np_, jp, nk),
            scratch(ni + 2, 3, jp, nk),
            scratch(ni + 2, jp, nk),
            scratch(ni + 2, 6, jp, nk),
            scratch(ni + 2, jp, nk),
            scratch(ni + 2, 3, jp, nk),
            scratch(ni + 2, 3, jp, nk),
            scratch(ni + 2, 3, jp, nk),
            scratch(ni + 2, 3, jp, nk),
            scratch(3, ni, nj, nk),
            scratch(3 * ni * nj, nk),
            scratch(ns, nk // ns, 3 * ni * nj),
            scratch(ns, nk // ns, 3 * ni * nj),
            scratch(STEPS, 2, np_ * nj, nk),
            scratch(STEPS, 2, np_ * nj, nk),
            scratch(STEPS, 2, ni, np_, nk),
            scratch(STEPS, 2, ni, np_, nk),
            scratch(2, 2 * nj, nk),
            scratch(2, 2 * nj, nk),
            scratch(2, ni, 2, nk),
            scratch(2, ni, 2, nk),
            scratch(ITERS, 2, 3 * nj, nk),
            scratch(ITERS, 2, 3 * nj, nk),
            scratch(ITERS, 2, ni, 3, nk),
            scratch(ITERS, 2, ni, 3, nk),
            pltpu.SemaphoreType.DMA((stages, 4)),
            pltpu.SemaphoreType.DMA((stages, 4)),
            pltpu.SemaphoreType.DMA((ns,)),
            pltpu.SemaphoreType.DMA((ns,)),
        ],
        compiler_params=pltpu.CompilerParams(
            collective_id=0, has_side_effects=True, vmem_limit_bytes=48 * 1024 * 1024
        ),
    )(phases, speeds, variants)
    return fields, jnp.transpose(moved, (0, 2, 1, 3))


def solution(mesh):
    placed = (P(None, "space", "slab", None), P(), P("space", "slab", None, None), P())
    return jax.shard_map(
        functools.partial(shards, mesh),
        mesh=mesh,
        in_specs=placed,
        out_specs=(P(None, "space", "slab", None), P(None, "space", "slab", None)),
        check_vma=False,
    )
```
